32 devices in a mesh: group: 8 (over z, x), ep: 4 (over y, core).
Axes of the slice: x: 2, y: 2, z: 4, core: 2. Of those that a mesh axis runs over, the one named last changes fastest.
Arguments:
- tokens: bfloat16 [256, 2048], P('group'), may hold values from -6 to 6
- prefill_states: float32 [64, 32, 128, 128], P('group', 'ep'), may hold values from -3 to 3
- prefill_tails: bfloat16 [64, 3, 8192], P('group', None, 'ep'), may hold values from -6 to 6
- src_group: int32 [8, 8], replicated, may hold values from 0 to 7, as said below
- src_slot: int32 [8, 8], replicated, may hold values from 0 to 7, as said below
- in_gain: float32 [2048], replicated, may hold values from 0.5 to 1.5
- w_qkvz: bfloat16 [2048, 12288], P(None, 'ep'), may hold values from -0.125 to 0.125
- w_ba: bfloat16 [2048, 64], P(None, 'ep'), may hold values from -0.125 to 0.125
- conv_weight: float32 [4, 8192], P(None, 'ep'), may hold values from -3 to 3
- a_log: float32 [32], P('ep'), may hold values from -4 to -1
- dt_bias: float32 [32], P('ep'), may hold values from -5 to -2
- norm_gain: float32 [128], replicated, may hold values from 0.5 to 1.5
- w_out: bfloat16 [4096, 2048], P('ep'), may hold values from -0.09375 to 0.09375
- post_gain: float32 [2048], replicated, may hold values from 0.5 to 1.5
- expert_ids: int32 [256, 10], P('group'), may hold values from 0 to 31, all different within a row; in each aligned block of 32 rows (0 to 31, 32 to 63, ...) at most 16 rows name the same one
- gate_probs: float32 [256, 10], P('group'), may hold values from 0.02 to 0.3
- gate_up_weight: bfloat16 [32, 2048, 1024], P(('group', 'ep')), may hold values from -0.125 to 0.125
- down_weight: bfloat16 [32, 512, 2048], P(('group', 'ep')), may hold values from -0.25 to 0.25
Outputs:
- layer_out: bfloat16 [256, 2048], P('group', 'ep')
- new_states: float32 [64, 32, 128, 128], P('group', 'ep')
- new_tails: bfloat16 [64, 3, 8192], P('group', None, 'ep')
The draws below stay inside these ranges and needn't reach their ends.
Inputs may be any that keep to these rules, and one draw needn't show every extreme that they name: Every (prefill instance, slot) pair feeds exactly one decode slot. (src_group[d, j] - d) modulo 8 does not depend on d and takes 8 different values over the 8 slots of a decode group. With stride = 1: if stride is 1 these are all values below 8; else they are k * stride for k = 4 and (k * stride - 1) modulo 8 for every other k below 8. A decode group takes at most 1 request from one prefill instance, and some pair reaches it. `src_slot`: together with src_group, a permutation of all prefill slots. `expert_ids`: each row names 10 different experts; in the rows of one decode group no expert is named more than 16 times.
All inputs are finite; a program needn't handle non-finite values.
Results may differ from the reference program's by a relative error of at most 0.0075.
Values may be sent and summed in bfloat16 or wider, within the bound.
A program may use at most 192 MiB of HBM per device.

```python
import math
import jax
import jax.numpy as jnp
import numpy as np
from jax import lax

D = 2048
HEADS = 32
QK_HEADS = 16
KDIM = 128
VDIM = 128
FFE = 512
TOPK = 10
CONV = 4
R = 8
STEPS = 4
ROWS = 32
TOKENS = 256
BLOCK = 512
CH = 8192
EXPERTS = 32
CAP = 16
N_GROUP = 8


def offset_list(group_count, request_count):
    stride = group_count // request_count
    if stride == 1:
        return [which for which in range(request_count)]
    result = []
    for which in range(request_count):
        if which == request_count // 2:
            result.append(which * stride % group_count)
        else:
            result.append((which * stride - 1) % group_count)
    return result


def route_tables(key):
    slots_key = jax.random.fold_in(key, 1)
    order_key = jax.random.fold_in(key, 2)
    shuffle = jax.random.permutation(order_key, R).astype(jnp.int32)
    offset_base = jnp.array(offset_list(N_GROUP, R), dtype=jnp.int32)
    offset_table = offset_base[shuffle]
    sources = (jnp.arange(N_GROUP, dtype=jnp.int32)[:, None] + offset_table[None, :]) % N_GROUP
    slot_keys = jax.random.split(slots_key, N_GROUP)
    source_orders = jax.vmap(lambda one_key: jax.random.permutation(one_key, R))(slot_keys).astype(jnp.int32)
    columns = jnp.broadcast_to(jnp.arange(R, dtype=jnp.int32)[None, :], (N_GROUP, R))
    slots = source_orders[sources, columns]
    return (sources.astype(jnp.int32), slots.astype(jnp.int32))


def draw_src_group(key, part):
    tables = route_tables(key)
    return tables[0]


def draw_src_slot(key, part):
    tables = route_tables(key)
    return tables[1]


def draw_prefill_states(key, part):
    key = jax.random.fold_in(key, 5)
    base_key, sign_key, nudge_key = jax.random.split(key, 3)
    shape = (N_GROUP * R, HEADS, KDIM, VDIM)
    base = 0.5 * jnp.clip(jax.random.normal(base_key, shape, jnp.float32), -5.9, 5.9)
    coarse = base.astype(jnp.bfloat16).astype(jnp.float32)
    flips = jnp.where(jax.random.bernoulli(sign_key, 0.5, shape), 1.0, -1.0).astype(jnp.float32)
    nudge = jax.random.uniform(nudge_key, shape, jnp.float32, 0.0011, 0.0019)
    return coarse * (1.0 + flips * nudge)


def block_levels(rng, dims, cuts, smallest, high):
    def one(axis_at, blocks):
        steps = jax.random.uniform(jax.random.fold_in(jax.random.fold_in(rng, 6), axis_at), (blocks,), jnp.float32, smallest / len(cuts), high / len(cuts))
        return jnp.repeat(jnp.exp(steps), dims[axis_at] // blocks).reshape((-1,) + (1,) * (len(dims) - axis_at - 1))

    loudness = one(*cuts[0])
    for cut in cuts[1:]:
        loudness = loudness * one(*cut)
    return loudness


def assign_block(rng, own, number, rows, amount, top, bound, skew):
    order = jax.random.permutation(rng, amount)
    packed, ordinary = portions_of(amount, rows * top, bound, skew, True), portions_of(amount, rows * top, bound, skew, False)
    places = jnp.arange(amount)

    def named(lengths, turn):
        used = int((lengths > 0).sum())
        fixed = max(1, used // 4)
        moved = fixed + (places - fixed + turn * (used - fixed)) % max(1, amount - fixed)
        return jnp.zeros((amount,), jnp.int32).at[order[jnp.where(places < fixed, places, moved)]].set(jnp.asarray(lengths, jnp.int32))

    lengths = jnp.where(number % 4 == 0, named(packed, number // 4), named(ordinary, number - number // 4 - 1))
    mixed = jax.random.permutation(jax.random.fold_in(own, 3), amount)
    source_of, receiver = mixed[0:amount // 2 * 2:2], mixed[1:amount // 2 * 2:2]
    room = jnp.minimum(lengths[source_of] - 1, bound - lengths[receiver]) // 2
    room = jnp.where((source_of == order[0]) | (receiver == order[0]) | (lengths[receiver] == 0), 0, jnp.maximum(room, 0))
    moved = jax.random.randint(jax.random.fold_in(own, 4), (amount // 2,), 0, 1 << 20) % (room + 1)
    lengths = lengths.at[source_of].add(-moved).at[receiver].add(moved)
    labels = jnp.searchsorted(jnp.cumsum(lengths), jnp.arange(rows * top), side="right").astype(jnp.int32)
    table = labels.reshape(top, rows).T
    table = table[jax.random.permutation(jax.random.fold_in(own, 1), rows)]
    turn = jax.random.randint(jax.random.fold_in(own, 2), (rows, 1), 0, top)
    return jnp.take_along_axis(table, (jnp.arange(top)[None, :] + turn) % top, axis=1)


def portions_of(amount, total, bound, skew, full):
    weights = [(1 << 20) // math.isqrt(grade ** skew) + 1 for grade in range(1, amount + 1)]
    largest = bound if full else min(bound, max(-(-total // amount), total * weights[0] // sum(weights)))
    least = 1 if total - largest >= amount - 1 else 0
    holding, spare = [largest] + [least] * (amount - 1), total - largest - least * (amount - 1)
    while spare > 0:
        free = [i for i in range(1, amount) if holding[i] < largest] or [i for i in range(1, amount) if holding[i] < bound]
        mass, budget = sum([weights[i] for i in free]), spare
        for i in free:
            extra = min(bound - holding[i], max(1, budget * weights[i] // mass), spare)
            holding[i] = holding[i] + extra
            spare = spare - extra
    return np.array(holding)


def scatter_about(key, extent, deviation, reach, shards=(), kind=jnp.bfloat16):
    values = jax.random.normal(key, extent, jnp.float32) * deviation
    if len(shards) > 0:
        values = block_levels(key, extent, shards, -0.22, 0.18) * values
    return jnp.clip(values, min=-reach, max=reach).astype(kind)


def setup_inputs(seed: int = 0) -> dict:
    streams_of = jax.random.split(jax.random.key(seed), 19)
    tokens = scatter_about(streams_of[0], (TOKENS, D), 1.0, 6.0, ((0, 8),))
    prefill_states = draw_prefill_states(jax.random.fold_in(streams_of[18], 71), 0)
    prefill_tails = scatter_about(streams_of[2], (N_GROUP * R, CONV - 1, CH), 1.0, 6.0, ((0, 8), (2, 4)))
    src_group = draw_src_group(jax.random.fold_in(streams_of[18], 71), 0)
    src_slot = draw_src_slot(jax.random.fold_in(streams_of[18], 71), 0)
    in_gain = jnp.clip(1.0 + 0.1 * jax.random.normal(streams_of[5], (D,), jnp.float32), 0.5, 1.5)
    w_qkvz = scatter_about(streams_of[6], (D, QK_HEADS * (2 * KDIM + 4 * VDIM)), D ** -0.5, 0.125, ((1, 4),))
    w_ba = scatter_about(streams_of[7], (D, 2 * HEADS), D ** -0.5, 0.125, ((1, 4),))
    conv_weight = scatter_about(streams_of[8], (CONV, CH), 0.5, 3.0, ((1, 4),), jnp.float32)
    a_log = jnp.clip(-4.0 + 3.0 * jax.random.uniform(streams_of[9], (HEADS,), jnp.float32) ** block_levels(streams_of[9], (HEADS,), ((0, 4),), -0.2, 0.2), -4.0, -1.0)
    dt_bias = jnp.clip(-5.0 + 3.0 * jax.random.uniform(streams_of[10], (HEADS,), jnp.float32) ** block_levels(streams_of[10], (HEADS,), ((0, 4),), -0.2, 0.2), -5.0, -2.0)
    norm_gain = jnp.clip(1.0 + 0.1 * jax.random.normal(streams_of[11], (VDIM,), jnp.float32), 0.5, 1.5)
    w_out = scatter_about(streams_of[12], (HEADS * VDIM, D), (HEADS * VDIM) ** -0.5, 0.09375, ((0, 4),))
    post_gain = jnp.clip(1.0 + 0.1 * jax.random.normal(streams_of[13], (D,), jnp.float32), 0.5, 1.5)
    expert_ids_keys = jax.random.split(jax.random.fold_in(streams_of[14], 1), TOKENS // ROWS)
    expert_ids_turns = jax.random.permutation(jax.random.fold_in(streams_of[14], 3), TOKENS // ROWS)
    expert_ids = jax.vmap(lambda own, number: assign_block(jax.random.fold_in(streams_of[14], 2), own, number, ROWS, EXPERTS, TOPK, CAP, 2))(expert_ids_keys, expert_ids_turns).reshape((TOKENS, TOPK))
    gate_probs = jnp.clip(jnp.exp(math.log(0.3) - 2.7080503 * jax.random.uniform(streams_of[15], (TOKENS, TOPK), jnp.float32) ** block_levels(streams_of[15], (TOKENS, TOPK), ((0, 8),), -0.2, 0.2)), 0.02, 0.3)
    gate_up_weight = scatter_about(streams_of[16], (EXPERTS, D, 2 * FFE), D ** -0.5, 0.125, ((0, 32),))
    down_weight = scatter_about(streams_of[17], (EXPERTS, FFE, D), FFE ** -0.5, 0.25, ((0, 32),))
    return {"tokens": tokens, "prefill_states": prefill_states, "prefill_tails": prefill_tails, "src_group": src_group, "src_slot": src_slot, "in_gain": in_gain, "w_qkvz": w_qkvz, "w_ba": w_ba, "conv_weight": conv_weight, "a_log": a_log, "dt_bias": dt_bias, "norm_gain": norm_gain, "w_out": w_out, "post_gain": post_gain, "expert_ids": expert_ids, "gate_probs": gate_probs, "gate_up_weight": gate_up_weight, "down_weight": down_weight}


epsilon = 1e-06

def rms_norm(values, scale_factors):
    return values * lax.rsqrt(lax.optimization_barrier(jnp.mean(values * values, axis=-1, keepdims=True)) + epsilon) * scale_factors

def unit_norm(values):
    return values * lax.rsqrt(lax.optimization_barrier(jnp.sum(values * values, axis=-1, keepdims=True)) + epsilon)

def reference(tokens, prefill_states, prefill_tails, src_group, src_slot, in_gain, w_qkvz, w_ba, conv_weight, a_log, dt_bias, norm_gain, w_out, post_gain, expert_ids, gate_probs, gate_up_weight, down_weight):
    slots_all = N_GROUP * R
    highest = lax.Precision.HIGHEST
    source_rows = (src_group * R + src_slot).reshape(-1).astype(jnp.int32)
    memory = prefill_states[source_rows].reshape(slots_all, QK_HEADS, 2, KDIM, VDIM)
    conv_tails = prefill_tails[source_rows]
    input_rows = tokens.astype(jnp.float32)
    normed = rms_norm(input_rows, in_gain).astype(jnp.bfloat16)
    projected = jnp.dot(normed, w_qkvz, preferred_element_type=jnp.float32).reshape(slots_all, STEPS, QK_HEADS, 2 * KDIM + 4 * VDIM)
    rates = jnp.dot(normed, w_ba, preferred_element_type=jnp.float32).reshape(slots_all, STEPS, QK_HEADS, 4)
    conv_in = projected[..., :BLOCK].astype(jnp.bfloat16)
    gate_z = projected[..., BLOCK:].reshape(slots_all, STEPS, QK_HEADS, 2, VDIM)
    window = jnp.concatenate([conv_tails.reshape(slots_all, CONV - 1, QK_HEADS, BLOCK), conv_in], axis=1)
    new_tails = window[:, STEPS:].reshape(slots_all, CONV - 1, CH)
    window = window.astype(jnp.float32)
    taps = conv_weight.reshape(CONV, QK_HEADS, BLOCK)
    mixed = jnp.zeros((slots_all, STEPS, QK_HEADS, BLOCK), jnp.float32)
    for offset in range(CONV):
        mixed = mixed + taps[offset] * window[:, offset:offset + STEPS]
    conv_out = jax.nn.silu(mixed)
    queries = unit_norm(conv_out[..., :KDIM]) * KDIM ** (-0.5)
    keys = unit_norm(conv_out[..., KDIM:2 * KDIM])
    values = conv_out[..., 2 * KDIM:].reshape(slots_all, STEPS, QK_HEADS, 2, VDIM)
    write_rate = jax.nn.sigmoid(rates[..., :2])
    decay_rate = jnp.exp(-jnp.exp(a_log.reshape(QK_HEADS, 2)) * jax.nn.softplus(rates[..., 2:] + dt_bias.reshape(QK_HEADS, 2)))
    readouts = []
    for token_step in range(STEPS):
        memory = decay_rate[:, token_step, :, :, None, None] * memory
        predicted = jnp.einsum('rqk,rqhkv->rqhv', keys[:, token_step], memory, precision=highest)
        delta = write_rate[:, token_step, :, :, None] * (values[:, token_step] - predicted)
        memory = memory + jnp.einsum('rqk,rqhv->rqhkv', keys[:, token_step], delta, precision=highest)
        readouts.append(jnp.einsum('rqk,rqhkv->rqhv', queries[:, token_step], memory, precision=highest))
    readout = jnp.stack(readouts, axis=1)
    gated = (rms_norm(readout, norm_gain) * jax.nn.silu(gate_z)).astype(jnp.bfloat16).reshape(TOKENS, HEADS * VDIM)
    residual = input_rows + jnp.dot(gated, w_out, preferred_element_type=jnp.float32)
    moe_input = rms_norm(residual, post_gain).astype(jnp.bfloat16)
    assigned = ROWS * TOPK
    ids_group = expert_ids.reshape(N_GROUP, assigned)
    positions = jnp.arange(assigned, dtype=jnp.int32)
    earlier = positions[None, :] < positions[:, None]
    arrival = lax.optimization_barrier(jnp.sum(((ids_group[:, :, None] == ids_group[:, None, :]) & earlier[None]).astype(jnp.int32), axis=-1))
    slot_index = (jnp.arange(N_GROUP, dtype=jnp.int32)[:, None] * CAP + arrival).reshape(-1)
    token_index = jnp.broadcast_to(jnp.arange(TOKENS, dtype=jnp.int32).reshape(N_GROUP, ROWS, 1), (N_GROUP, ROWS, TOPK)).reshape(-1)
    ids_flat = ids_group.reshape(-1)
    table = jnp.zeros((EXPERTS, N_GROUP * CAP), jnp.int32).at[ids_flat, slot_index].set(token_index)

    def run_expert(pieces):
        gate_up, down, rows_used = pieces
        picked = moe_input[rows_used]
        paired_halves = jnp.dot(picked, gate_up, preferred_element_type=jnp.float32)
        hidden_state = (jax.nn.silu(paired_halves[:, :FFE]) * paired_halves[:, FFE:]).astype(jnp.bfloat16)
        return jnp.dot(hidden_state, down, preferred_element_type=jnp.float32).astype(jnp.bfloat16)
    expert_table = lax.map(run_expert, (gate_up_weight, down_weight, table))
    expert_rows = expert_table[ids_flat, slot_index].astype(jnp.float32).reshape(TOKENS, TOPK, D)
    layer_out = (residual + lax.optimization_barrier(jnp.sum(gate_probs[:, :, None] * expert_rows, axis=1))).astype(jnp.bfloat16)
    new_states = memory.reshape(slots_all, HEADS, KDIM, VDIM)
    return (layer_out, new_states, new_tails)
```

```python
import jax
import jax.numpy as jnp
from jax import lax
from jax.sharding import PartitionSpec as P

epsilon = 1e-06


def rms_norm(values, scale_factors):
    return (
        values
        * lax.rsqrt(jnp.mean(values * values, axis=-1, keepdims=True) + epsilon)
        * scale_factors
    )


def unit_norm(values):
    return values * lax.rsqrt(jnp.sum(values * values, axis=-1, keepdims=True) + epsilon)


def body(
    tokens,
    prefill_states,
    prefill_tails,
    src_group,
    src_slot,
    in_gain,
    w_qkvz,
    w_ba,
    conv_weight,
    a_log,
    dt_bias,
    norm_gain,
    w_out,
    post_gain,
    expert_ids,
    gate_probs,
    gate_up_weight,
    down_weight,
):
    groups = lax.axis_size("group")
    shards = lax.axis_size("ep")
    my_group = lax.axis_index("group")
    my_column = lax.axis_index("ep")
    highest = lax.Precision.HIGHEST
    requests = prefill_states.shape[0]
    head_pairs = w_ba.shape[1] // 4
    key_size = prefill_states.shape[2]
    value_size = prefill_states.shape[3]
    block_width = 2 * key_size + 2 * value_size
    taps_count = conv_weight.shape[0]
    row_count = tokens.shape[0]
    steps_count = row_count // requests
    model_width = tokens.shape[1]
    share_width = model_width // shards
    stride = groups // requests
    offsets = [
        which * stride if stride == 1 or which == requests // 2 else (which * stride - 1) % groups
        for which in range(requests)
    ]
    slot_offsets = (src_group[0] % groups).astype(jnp.int32)
    kept_states = prefill_states.astype(jnp.bfloat16)
    state_pieces = []
    tail_pieces = []
    for offset in offsets:
        target = (my_group - offset) % groups
        which = jnp.argmax(slot_offsets == offset)
        slot = src_slot[target, which]
        state_piece = lax.dynamic_index_in_dim(kept_states, slot, 0, keepdims=False)
        tail_piece = lax.dynamic_index_in_dim(prefill_tails, slot, 0, keepdims=False)
        if offset:
            pairs = [(source, (source - offset) % groups) for source in range(groups)]
            tail_piece = lax.ppermute(tail_piece, "group", pairs)
            state_piece = lax.ppermute(state_piece, "group", pairs)
        state_pieces.append(state_piece)
        tail_pieces.append(tail_piece)
    arrived = jnp.argmax(slot_offsets[:, None] == jnp.array(offsets)[None, :], axis=1)
    states_next = jnp.stack(state_pieces)[arrived].astype(jnp.float32)
    tails_next = jnp.stack(tail_pieces)[arrived]
    input_rows = tokens.astype(jnp.float32)
    normed = rms_norm(input_rows, in_gain).astype(jnp.bfloat16)
    projected = jnp.dot(normed, w_qkvz, preferred_element_type=jnp.float32).reshape(
        requests, steps_count, head_pairs, block_width + 2 * value_size
    )
    rates = jnp.dot(normed, w_ba, preferred_element_type=jnp.float32).reshape(
        requests, steps_count, head_pairs, 4
    )
    conv_in = projected[..., :block_width].astype(jnp.bfloat16)
    gate_z = projected[..., block_width:].reshape(requests, steps_count, head_pairs, 2, value_size)
    window = jnp.concatenate(
        [tails_next.reshape(requests, taps_count - 1, head_pairs, block_width), conv_in], axis=1
    )
    new_tails = window[:, steps_count:].reshape(requests, taps_count - 1, head_pairs * block_width)
    window = window.astype(jnp.float32)
    taps = conv_weight.reshape(taps_count, head_pairs, block_width)
    mixed = jnp.zeros((requests, steps_count, head_pairs, block_width), jnp.float32)
    for offset in range(taps_count):
        mixed = mixed + taps[offset] * window[:, offset : offset + steps_count]
    conv_out = jax.nn.silu(mixed)
    queries = unit_norm(conv_out[..., :key_size]) * key_size ** (-0.5)
    keys = unit_norm(conv_out[..., key_size : 2 * key_size])
    values = conv_out[..., 2 * key_size :].reshape(requests, steps_count, head_pairs, 2, value_size)
    write_rate = jax.nn.sigmoid(rates[..., :2])
    decay_rate = jnp.exp(
        -jnp.exp(a_log.reshape(head_pairs, 2))
        * jax.nn.softplus(rates[..., 2:] + dt_bias.reshape(head_pairs, 2))
    )
    memory = states_next.reshape(requests, head_pairs, 2, key_size, value_size)
    readouts = []
    for token_step in range(steps_count):
        memory = decay_rate[:, token_step, :, :, None, None] * memory
        predicted = jnp.einsum("rqk,rqhkv->rqhv", keys[:, token_step], memory, precision=highest)
        delta = write_rate[:, token_step, :, :, None] * (values[:, token_step] - predicted)
        memory = memory + jnp.einsum(
            "rqk,rqhv->rqhkv", keys[:, token_step], delta, precision=highest
        )
        readouts.append(
            jnp.einsum("rqk,rqhkv->rqhv", queries[:, token_step], memory, precision=highest)
        )
    readout = jnp.stack(readouts, axis=1)
    gated = (
        (rms_norm(readout, norm_gain) * jax.nn.silu(gate_z))
        .astype(jnp.bfloat16)
        .reshape(row_count, head_pairs * 2 * value_size)
    )
    head_part = jnp.dot(gated, w_out, preferred_element_type=jnp.float32)
    new_states = memory.reshape(requests, head_pairs * 2, key_size, value_size)
    residual = input_rows + lax.psum(head_part, "ep")
    moe_input = rms_norm(residual, post_gain).astype(jnp.bfloat16)
    residual_share = lax.dynamic_slice_in_dim(residual, my_column * share_width, share_width, 1)
    local_experts = gate_up_weight.shape[0]
    hidden_width = down_weight.shape[1]
    top_count = expert_ids.shape[1]
    experts_all = local_experts * groups * shards
    capacity = max(2, (row_count * top_count * 8 + experts_all * 5 - 1) // (experts_all * 5))
    slot_total = local_experts * groups * capacity
    ids_flat = expert_ids.reshape(-1)
    assigned = ids_flat.shape[0]
    positions = jnp.arange(assigned, dtype=jnp.int32)
    earlier_pick = positions[None, :] < positions[:, None]
    arrival = jnp.sum(
        ((ids_flat[:, None] == ids_flat[None, :]) & earlier_pick).astype(jnp.int32), axis=1
    )
    on_column = ids_flat // local_experts % shards == my_column
    dest_group = ids_flat // (shards * local_experts)
    local_slot = ids_flat % local_experts
    slot_id = (local_slot * groups + dest_group) * capacity + arrival
    slot_match = on_column[None, :] & (
        slot_id[None, :] == jnp.arange(slot_total, dtype=jnp.int32)[:, None]
    )
    slot_match = slot_match.reshape(slot_total, row_count, top_count)
    pick_matrix = jnp.any(slot_match, axis=-1).astype(jnp.bfloat16)
    weight_matrix = jnp.sum(jnp.where(slot_match, gate_probs[None, :, :], 0.0), axis=-1)
    send_rows = jnp.dot(pick_matrix, moe_input, preferred_element_type=jnp.float32).astype(
        jnp.bfloat16
    )
    send_rows = send_rows.reshape(local_experts, groups, capacity, model_width)
    received_rows = lax.all_to_all(
        send_rows, "group", split_axis=1, concat_axis=1, tiled=True
    ).reshape(local_experts, groups * capacity, model_width)
    paired_halves = jnp.einsum(
        "esp,epk->esk", received_rows, gate_up_weight, preferred_element_type=jnp.float32
    )
    hidden_state = (
        jax.nn.silu(paired_halves[..., :hidden_width]) * paired_halves[..., hidden_width:]
    ).astype(jnp.bfloat16)
    expert_rows = jnp.einsum(
        "ugh,uhv->ugv", hidden_state, down_weight, preferred_element_type=jnp.float32
    ).astype(jnp.bfloat16)
    expert_rows = expert_rows.reshape(local_experts, groups, capacity, model_width)
    returned = lax.all_to_all(
        expert_rows, "group", split_axis=1, concat_axis=1, tiled=True
    ).reshape(slot_total, model_width)
    weighted = jnp.dot(weight_matrix.T, returned.astype(jnp.float32), precision=highest)
    expert_share = lax.psum_scatter(
        weighted.astype(jnp.bfloat16), "ep", scatter_dimension=1, tiled=True
    ).astype(jnp.float32)
    layer_out = (residual_share + expert_share).astype(jnp.bfloat16)
    return (layer_out, new_states, new_tails)


def solution(mesh):
    in_specs = (
        P("group", None),
        P("group", "ep", None, None),
        P("group", None, "ep"),
        P(),
        P(),
        P(),
        P(None, "ep"),
        P(None, "ep"),
        P(None, "ep"),
        P("ep"),
        P("ep"),
        P(),
        P("ep", None),
        P(),
        P("group", None),
        P("group", None),
        P(("group", "ep"), None, None),
        P(("group", "ep"), None, None),
    )
    out_specs = (P("group", "ep"), P("group", "ep", None, None), P("group", None, "ep"))
    return jax.shard_map(body, mesh=mesh, in_specs=in_specs, out_specs=out_specs, check_vma=False)
```

```python
import functools
import jax
import jax.numpy as jnp
from jax import lax
from jax.experimental import pallas as pl
from jax.experimental.pallas import tpu as pltpu
from jax.sharding import PartitionSpec as P

epsilon = 1e-06
MESH = pl.DeviceIdType.MESH
bf16, f32 = jnp.bfloat16, jnp.float32


def silu(x):
    return x * (1.0 / (1.0 + jnp.exp(-x)))


def kernel(
    G, E, offsets, S,
    slot_ref, tok_ref, own_ref, wts_ref, tails_ref, gain_ref, wba_ref, conv_ref, alog_ref, dtb_ref,
    ngain_ref, pgain_ref, sel_ref, wq_hbm, wo_hbm, gu_hbm, dn_hbm, st_hbm,
    lay_ref, ct_ref, st_out,
    wq, wo, gu, dn, st, st_send, st_recv, st_new, tok_recv, wts_all, x_ref, nrm, gated,
    ck_send, ck_recv, hp_send, hp_recv, res, moe, hidden, hid, y_send, y_recv, base, part, z_recv,
    load_sem, out_sem, tok_ss, tok_rs, st_ss, st_rs, ck_ss, ck_rs, w_ss, w_rs,
    hp_ss, hp_rs, g_ss, g_rs, e_ss, e_rs, y_ss, y_rs, z_ss, z_rs,
):
    R = len(offsets)
    ROWS = S * R
    HP = conv_ref.shape[1] // 512
    HV = 2 * HP
    L = gu.shape[0]
    D = x_ref.shape[1]
    F = dn.shape[1]
    share = D // E
    g = lax.axis_index("group")
    e = lax.axis_index("ep")

    loads = [
        pltpu.make_async_copy(src, dst, load_sem.at[n])
        for n, (src, dst) in enumerate(
            [(st_hbm, st), (wq_hbm, wq), (wo_hbm, wo), (gu_hbm, gu), (dn_hbm, dn)]
        )
    ]
    for copy in loads:
        copy.start()

    barrier = pltpu.get_barrier_semaphore()

    def greet_group(k, carry):
        pl.semaphore_signal(barrier, inc=1, device_id=(lax.rem(g + k, G), e), device_id_type=MESH)
        return carry

    def greet_ep(m, carry):
        pl.semaphore_signal(barrier, inc=1, device_id=(g, lax.rem(e + m, E)), device_id_type=MESH)
        return carry

    lax.fori_loop(1, G, greet_group, 0)
    lax.fori_loop(1, E, greet_ep, 0)
    pl.semaphore_wait(barrier, G - 1 + E - 1)

    def move(src, dst, ss, rs, i, group):
        if offsets[i] % G == 0:
            return pltpu.make_async_copy(src, dst, rs.at[i]), False
        return (
            pltpu.make_async_remote_copy(
                src_ref=src, dst_ref=dst, send_sem=ss.at[i], recv_sem=rs.at[i],
                device_id=(group, e), device_id_type=MESH,
            ),
            True,
        )

    def finish(copies):
        for copy, _ in copies:
            copy.wait()

    tok_copies = []
    for i in range(R):
        rows = pl.ds(16 * i, 16)
        pair = move(tok_ref.at[rows], tok_recv.at[rows], tok_ss, tok_rs, i, lax.rem(g + offsets[i], G))
        pair[0].start()
        tok_copies.append(pair)

    def wts_copy(k):
        to = lax.rem(g + k, G)
        return pltpu.make_async_remote_copy(
            src_ref=wts_ref.at[to], dst_ref=wts_all.at[k], send_sem=w_ss.at[k], recv_sem=w_rs.at[k],
            device_id=(to, e), device_id_type=MESH,
        )

    lax.fori_loop(1, G, lambda k, c: (wts_copy(k).start(), c)[1], 0)
    wts_all[0] = wts_ref[g]

    loads[0].wait()
    st_copies = []
    for i in range(R):
        st_send[i] = st[slot_ref[i]].astype(bf16)
        pair = move(st_send.at[i], st_recv.at[i], st_ss, st_rs, i, lax.rem(g + G - offsets[i], G))
        pair[0].start()
        st_copies.append(pair)

    finish(tok_copies)
    parts = sel_ref.shape[0]
    width = D // parts
    for q in range(parts):
        x_ref[:, q * width : (q + 1) * width] = jnp.dot(
            sel_ref[q], tok_recv[...], preferred_element_type=f32
        )

    def normalize(x, gain):
        return x * lax.rsqrt(jnp.mean(x * x, axis=-1, keepdims=True) + epsilon) * gain

    nrm[:ROWS] = normalize(x_ref[...], gain_ref[...]).astype(bf16)
    nrm[ROWS:] = normalize(own_ref[...].astype(f32), gain_ref[...]).astype(bf16)

    rates = jnp.dot(nrm[:ROWS], wba_ref[...], preferred_element_type=f32)
    write_rate = 1.0 / (1.0 + jnp.exp(-rates))
    shifted = rates + dtb_ref[...]
    softplus = jnp.maximum(shifted, 0.0) + jnp.log1p(jnp.exp(-jnp.abs(shifted)))
    decays = jnp.exp(-jnp.exp(alog_ref[...]) * softplus)
    request_of = lax.broadcasted_iota(jnp.int32, (2 * ROWS, 128), 0) % R

    loads[1].wait()
    for h in range(HP):
        projected = jnp.dot(nrm[...], wq[:, h * 768 : (h + 1) * 768], preferred_element_type=f32)
        rounded = projected[:, :512].astype(bf16)
        ct_ref[:, h * 512 : (h + 1) * 512] = rounded[ROWS:]
        entered = rounded[:ROWS].astype(f32)
        window = [tails_ref[n][:, h * 512 : (h + 1) * 512] for n in range(3)]
        window += [entered[s * R : (s + 1) * R] for s in range(S)]
        taps = [conv_ref[n : n + 1, h * 512 : (h + 1) * 512] for n in range(4)]
        ks, qs, vs = [], [], []
        for s in range(S):
            mixed = taps[0] * window[s]
            for n in range(1, 4):
                mixed = mixed + taps[n] * window[s + n]
            out = silu(mixed)
            q_, k_ = out[:, :128], out[:, 128:256]
            qs.append(q_ * lax.rsqrt(jnp.sum(q_ * q_, axis=-1, keepdims=True) + epsilon) * 128 ** (-0.5))
            ks.append(k_ * lax.rsqrt(jnp.sum(k_ * k_, axis=-1, keepdims=True) + epsilon))
            vs.append(out[:, 256:])
        both = jnp.concatenate(ks + qs, axis=0).astype(bf16)
        kk = {(t, s): jnp.sum(ks[t] * ks[s], axis=-1, keepdims=True) for s in range(S) for t in range(s)}
        kq = {(t, s): jnp.sum(ks[t] * qs[s], axis=-1, keepdims=True) for s in range(S) for t in range(s + 1)}
        for s in range(S):
            for i in range(R):
                row = S * HV + h * S + s
                ck_send[i, row : row + 1, :] = ks[s][i : i + 1]
        for p in range(2):
            hv = 2 * h + p

            def apply(i, acc):
                product = jnp.dot(both, st_send[i, hv], preferred_element_type=f32)
                return jnp.where(request_of == i, product, acc)

            start = lax.fori_loop(0, R, apply, jnp.zeros((2 * ROWS, 128), f32))
            dec = [decays[s * R : (s + 1) * R, 4 * h + 2 + p : 4 * h + 3 + p] for s in range(S)]
            beta = [write_rate[s * R : (s + 1) * R, 4 * h + p : 4 * h + p + 1] for s in range(S)]
            kept = []
            total = None
            for s in range(S):
                total = dec[s] if total is None else total * dec[s]
                kept = [c * dec[s] for c in kept]
                guess = total * start[s * R : (s + 1) * R]
                for t in range(s):
                    guess = guess + kk[t, s] * kept[t]
                kept.append(beta[s] * (vs[s][:, p * 128 : (p + 1) * 128] - guess))
                read = total * start[ROWS + s * R : ROWS + (s + 1) * R]
                for t in range(s + 1):
                    read = read + kq[t, s] * kept[t]
                z = projected[s * R : (s + 1) * R, 512 + p * 128 : 640 + p * 128]
                gated[s * R : (s + 1) * R, hv * 128 : (hv + 1) * 128] = (
                    normalize(read, ngain_ref[...]) * silu(z)
                )
            spread = jnp.broadcast_to(total, (R, 128))
            for i in range(R):
                for s in range(S):
                    ck_send[i, hv * S + s : hv * S + s + 1, :] = kept[s][i : i + 1]
                row = S * HV + S * HP + hv
                ck_send[i, row : row + 1, :] = spread[i : i + 1]
    used = S * HV + S * HP + HV
    if used < ck_send.shape[1]:
        for i in range(R):
            ck_send[i, used:, :] = jnp.zeros((ck_send.shape[1] - used, 128), f32)

    loads[2].wait()
    gated16 = gated[...].astype(bf16)
    for q in range(E):
        out = jnp.dot(gated16, wo[:, q * share : (q + 1) * share], preferred_element_type=f32)
        res[q] = x_ref[:, q * share : (q + 1) * share] + out
        hp_send[q] = out.astype(bf16)

    def hp_copy(m):
        return pltpu.make_async_remote_copy(
            src_ref=hp_send, dst_ref=hp_recv.at[m - 1], send_sem=hp_ss.at[m - 1],
            recv_sem=hp_rs.at[m - 1], device_id=(g, lax.rem(e + m, E)), device_id_type=MESH,
        )

    for m in range(1, E):
        hp_copy(m).start()
    ck_copies = []
    for i in range(R):
        pair = move(ck_send.at[i], ck_recv.at[i], ck_ss, ck_rs, i, lax.rem(g + G - offsets[i], G))
        pair[0].start()
        ck_copies.append(pair)
    for m in range(1, E):
        hp_copy(m).wait()
    square = jnp.zeros((ROWS, 1), f32)
    for q in range(E):
        value = res[q]
        for m in range(1, E):
            value = value + hp_recv[m - 1, q].astype(f32)
        res[q] = value
        square = square + jnp.sum(value * value, axis=-1, keepdims=True)
    scale = lax.rsqrt(square / D + epsilon)

    def rows_of(block):
        return pl.ds(pl.multiple_of(block * ROWS, ROWS), ROWS)

    moe[e, rows_of(g)] = (res[e] * scale * pgain_ref[e]).astype(bf16)

    def group_copy(k):
        place = moe.at[e, rows_of(g)]
        return pltpu.make_async_remote_copy(
            src_ref=place, dst_ref=place, send_sem=g_ss.at[k], recv_sem=g_rs.at[k],
            device_id=(lax.rem(g + k, G), e), device_id_type=MESH,
        )

    def arrived(k):
        place = moe.at[e, rows_of(lax.rem(g + G - k, G))]
        return pltpu.make_async_remote_copy(
            src_ref=place, dst_ref=place, send_sem=g_ss.at[k], recv_sem=g_rs.at[k],
            device_id=(lax.rem(g + k, G), e), device_id_type=MESH,
        )

    def pass_on(k, m):
        place = moe.at[e, rows_of(lax.rem(g + G - k, G))]
        return pltpu.make_async_remote_copy(
            src_ref=place, dst_ref=place, send_sem=e_ss.at[m - 1, k], recv_sem=e_rs.at[m - 1, k],
            device_id=(g, lax.rem(e + m, E)), device_id_type=MESH,
        )

    def taken(k, m):
        place = moe.at[lax.rem(e + E - m, E), rows_of(lax.rem(g + G - k, G))]
        return pltpu.make_async_remote_copy(
            src_ref=place, dst_ref=place, send_sem=e_ss.at[m - 1, k], recv_sem=e_rs.at[m - 1, k],
            device_id=(g, lax.rem(e + m, E)), device_id_type=MESH,
        )

    lax.fori_loop(1, G, lambda k, c: (group_copy(k).start(), c)[1], 0)
    for m in range(1, E):
        pass_on(0, m).start()

    base[...] = jnp.zeros_like(base)
    row_request = lax.broadcasted_iota(jnp.int32, (ROWS, share), 0) % R
    for i in range(R):
        base[lax.rem(g + G - offsets[i], G)] += jnp.where(row_request == i, res[e], 0.0)

    def forward(k, carry):
        arrived(k).wait_recv()
        for m in range(1, E):
            pass_on(k, m).start()
        return carry

    lax.fori_loop(1, G, forward, 0)

    def collect(k, carry):
        for m in range(1, E):
            taken(k, m).wait_recv()
        return carry

    lax.fori_loop(0, G, collect, 0)
    loads[3].wait()
    loads[4].wait()
    for l in range(L):
        halves = jnp.dot(moe[0], gu[l, :share], preferred_element_type=f32)
        for q in range(1, E):
            halves = halves + jnp.dot(
                moe[q], gu[l, q * share : (q + 1) * share], preferred_element_type=f32
            )
        hidden[l] = silu(halves[:, :F]) * halves[:, F:]
    row_hidden = lax.broadcasted_iota(jnp.int32, (ROWS, F), 0) % R

    def regroup(d, carry):
        for l in range(L):
            total = jnp.zeros((ROWS, F), f32)
            for i in range(R):
                total = jnp.where(
                    row_hidden == i, hidden[l, rows_of(lax.rem(d + offsets[i], G))], total
                )
            hid[l, rows_of(d)] = total.astype(bf16)
        return carry

    lax.fori_loop(0, G, regroup, 0)

    lax.fori_loop(1, G, lambda k, c: (wts_copy(k).wait(), c)[1], 0)
    picked = lax.broadcasted_iota(jnp.int32, (ROWS, 128), 0) == lax.broadcasted_iota(
        jnp.int32, (ROWS, 128), 1
    )
    for q in range(E):
        for l in range(L):
            out = jnp.dot(hid[l], dn[l, :, q * share : (q + 1) * share], preferred_element_type=f32)
            hidden_rows = out.astype(bf16).astype(f32)
            if l == 0:
                sums = [0.0] * G
            for d in range(G):
                tile = wts_all[lax.rem(g + G - d, G)]
                weight = jnp.sum(jnp.where(picked, tile[l : l + 1], 0.0), axis=-1, keepdims=True)
                sums[d] = sums[d] + weight * hidden_rows[d * ROWS : (d + 1) * ROWS]
        for d in range(G):
            y_send[q, d * ROWS : (d + 1) * ROWS] = sums[d].astype(bf16)

    def y_copy(k, m):
        d = lax.rem(g + k, G)
        to = lax.rem(e + m, E)
        return pltpu.make_async_remote_copy(
            src_ref=y_send.at[to, rows_of(d)], dst_ref=y_recv.at[m - 1, rows_of(d)],
            send_sem=y_ss.at[m - 1, k], recv_sem=y_rs.at[m - 1, k],
            device_id=(g, to), device_id_type=MESH,
        )

    def z_copy(k):
        to = lax.rem(g + k, G)
        return pltpu.make_async_remote_copy(
            src_ref=part.at[to], dst_ref=z_recv.at[k], send_sem=z_ss.at[k], recv_sem=z_rs.at[k],
            device_id=(to, e), device_id_type=MESH,
        )

    def y_start(k, carry):
        for m in range(1, E):
            y_copy(lax.rem(k, G), m).start()
        return carry

    lax.fori_loop(1, G + 1, y_start, 0)

    def y_total(k):
        d = lax.rem(g + k, G)
        total = base[d] + y_send[e, rows_of(d)].astype(f32)
        for m in range(1, E):
            y_copy(k, m).wait_recv()
            total = total + y_recv[m - 1, rows_of(d)].astype(f32)
        return total

    def combine(k, carry):
        part[lax.rem(g + k, G)] = y_total(k).astype(bf16)
        z_copy(k).start()
        return carry

    lax.fori_loop(1, G, combine, 0)
    final = y_total(0)

    finish(ck_copies)
    finish(st_copies)

    def put(i):
        return pltpu.make_async_copy(st_new.at[i], st_out.at[i], out_sem.at[i])

    def renew(i, carry):
        for hv in range(HV):
            h = hv // 2
            k4 = ck_recv[i, S * HV + h * S : S * HV + (h + 1) * S]
            c4 = ck_recv[i, hv * S : (hv + 1) * S]
            row = S * HV + S * HP + hv
            change = lax.dot_general(k4, c4, (((0,), (0,)), ((), ())), preferred_element_type=f32)
            st_new[i, hv] = ck_recv[i, row : row + 1] * st_recv[i, hv].astype(f32) + change
        put(i).start()
        return carry

    lax.fori_loop(0, R, renew, 0)
    for k in range(1, G):
        z_copy(k).wait_recv()
        final = final + z_recv[k].astype(f32)
    lay_ref[...] = final.astype(bf16)

    def drain(k, carry):
        group_copy(k).wait_send()
        z_copy(k).wait_send()
        return carry

    lax.fori_loop(1, G, drain, 0)

    def drain_ep(k, carry):
        for m in range(1, E):
            pass_on(k, m).wait_send()
            y_copy(k, m).wait_send()
        return carry

    lax.fori_loop(0, G, drain_ep, 0)
    lax.fori_loop(0, R, lambda i, c: (put(i).wait(), c)[1], 0)


def body(
    tokens, prefill_states, prefill_tails, src_group, src_slot, in_gain, w_qkvz, w_ba, conv_weight,
    a_log, dt_bias, norm_gain, w_out, post_gain, expert_ids, gate_probs, gate_up_weight, down_weight,
):
    G = lax.axis_size("group")
    E = lax.axis_size("ep")
    g = lax.axis_index("group")
    e = lax.axis_index("ep")
    R, HV = prefill_states.shape[:2]
    ROWS, D = tokens.shape
    S = ROWS // R
    HP = HV // 2
    L = gate_up_weight.shape[0]
    F = down_weight.shape[1]
    C = conv_weight.shape[1]
    share = D // E
    stride = G // R
    offsets = [
        which * stride if stride == 1 or which == R // 2 else (which * stride - 1) % G
        for which in range(R)
    ]
    offset_array = jnp.array(offsets, jnp.int32)
    slot_offsets = (src_group[0] % G).astype(jnp.int32)
    matches = (slot_offsets[:, None] == offset_array[None, :]).astype(jnp.int32)
    request_at = jnp.argmax(matches, axis=0)
    place_of = jnp.argmax(matches, axis=1)
    slots = src_slot[(g - offset_array) % G, request_at].astype(jnp.int32)

    parts = 16 // S
    ordered = tokens.reshape(R, S, D)[request_at]
    tok = ordered.reshape(R * 16, D // parts)
    rows = jnp.arange(ROWS)
    source = (rows % R) * 16 + (rows // R) * parts
    sel = (
        (source[None, :, None] + jnp.arange(parts)[:, None, None]) == jnp.arange(R * 16)[None, None, :]
    ).astype(bf16)

    expert_of = (jnp.arange(G)[:, None] * E + e) * L + jnp.arange(L)[None, :]
    hits = expert_ids[None, None] == expert_of[:, :, None, None]
    dense = jnp.sum(jnp.where(hits, gate_probs[None, None], 0.0), axis=-1)
    dense = dense.reshape(G, L, R, S)[:, :, request_at].transpose(0, 1, 3, 2).reshape(G, L, ROWS)
    wts = jnp.pad(dense, ((0, 0), (0, 8 - L), (0, 128 - ROWS)))

    tails = prefill_tails[slots].transpose(1, 0, 2).astype(f32)
    zero = jnp.zeros((HP, 2), f32)
    alog = jnp.concatenate([zero, a_log.reshape(HP, 2)], axis=1).reshape(1, 4 * HP)
    dtb = jnp.concatenate([zero, dt_bias.reshape(HP, 2)], axis=1).reshape(1, 4 * HP)

    ck_rows = -(-(S * HV + S * HP + HV) // 8) * 8
    vm = pl.BlockSpec(memory_space=pltpu.VMEM)
    anywhere = pl.BlockSpec(memory_space=pl.ANY)
    dma = pltpu.SemaphoreType.DMA
    V = pltpu.VMEM
    layer, conv_rows, states = pl.pallas_call(
        functools.partial(kernel, G, E, tuple(offsets), S),
        out_shape=(
            jax.ShapeDtypeStruct((ROWS, share), bf16),
            jax.ShapeDtypeStruct((ROWS, C), bf16),
            jax.ShapeDtypeStruct(prefill_states.shape, f32),
        ),
        in_specs=[pl.BlockSpec(memory_space=pltpu.SMEM)] + [vm] * 12 + [anywhere] * 5,
        out_specs=(vm, vm, anywhere),
        scratch_shapes=[
            V(w_qkvz.shape, bf16), V(w_out.shape, bf16), V(gate_up_weight.shape, bf16),
            V(down_weight.shape, bf16), V(prefill_states.shape, f32),
            V(prefill_states.shape, bf16), V(prefill_states.shape, bf16), V(prefill_states.shape, f32),
            V(tok.shape, bf16), V((G, 8, 128), f32), V((ROWS, D), f32), V((2 * ROWS, D), bf16),
            V((ROWS, HV * 128), f32), V((R, ck_rows, 128), f32), V((R, ck_rows, 128), f32),
            V((E, ROWS, share), bf16), V((E - 1, E, ROWS, share), bf16), V((E, ROWS, share), f32),
            V((E, G * ROWS, share), bf16), V((L, G * ROWS, F), f32), V((L, G * ROWS, F), bf16),
            V((E, G * ROWS, share), bf16), V((E - 1, G * ROWS, share), bf16),
            V((G, ROWS, share), f32), V((G, ROWS, share), bf16), V((G, ROWS, share), bf16),
            dma((5,)), dma((R,)), dma((R,)), dma((R,)), dma((R,)), dma((R,)), dma((R,)), dma((R,)),
            dma((G,)), dma((G,)), dma((E - 1,)), dma((E - 1,)), dma((G,)), dma((G,)),
            dma((E - 1, G)), dma((E - 1, G)), dma((E - 1, G)), dma((E - 1, G)), dma((G,)), dma((G,)),
        ],
        compiler_params=pltpu.CompilerParams(
            collective_id=0, has_side_effects=True, vmem_limit_bytes=58 * 2**20
        ),
    )(
        slots, tok, tokens, wts, tails, in_gain.reshape(1, D), w_ba, conv_weight, alog, dtb,
        norm_gain.reshape(1, 128), post_gain.reshape(E, 1, share), sel,
        w_qkvz, w_out, gate_up_weight, down_weight, prefill_states,
    )
    layer_out = layer.reshape(S, R, share)[:, place_of].transpose(1, 0, 2).reshape(ROWS, share)
    new_tails = conv_rows.reshape(R, S, C)[:, S - 3 :]
    return (layer_out, states[place_of], new_tails)


def solution(mesh):
    in_specs = (
        P("group", None), P("group", "ep", None, None), P("group", None, "ep"), P(), P(), P(),
        P(None, "ep"), P(None, "ep"), P(None, "ep"), P("ep"), P("ep"), P(), P("ep", None), P(),
        P("group", None), P("group", None), P(("group", "ep"), None, None),
        P(("group", "ep"), None, None),
    )
    out_specs = (P("group", "ep"), P("group", "ep", None, None), P("group", None, "ep"))
    return jax.shard_map(body, mesh=mesh, in_specs=in_specs, out_specs=out_specs, check_vma=False)
```

```python
import functools
import jax
import jax.numpy as jnp
from jax import lax
from jax.experimental import pallas as pl
from jax.experimental.pallas import tpu as pltpu
from jax.sharding import PartitionSpec as P

epsilon = 1e-06
MESH = pl.DeviceIdType.MESH
bf16, f32 = jnp.bfloat16, jnp.float32


def silu(x):
    return x * (1.0 / (1.0 + jnp.exp(-x)))


def kernel(
    G, E, offsets, S,
    sgroup_ref, sslot_ref, alog_ref, dtb_ref, own_ref, ids_ref, probs_ref, tail_ref, gain_ref, wba_ref,
    conv_ref, ngain_ref, pgain_ref, wq_hbm, wo_hbm, gu_hbm, dn_hbm, st_hbm,
    lay_ref, ct_ref, st_recv, ck_recv,
    wq, wo, gu, dn, st, st_send, own32, tok_ref, tails_ref, wts_ref, tok_recv, wts_all, x_ref, nrm,
    gated, ck_send, hp_send, hp_recv, res, pgain, moe, hidden, hid, y_send, y_recv, base, part, z_recv,
    load_sem, tok_ss, tok_rs, st_ss, st_rs, ck_ss, ck_rs, w_ss, w_rs,
    hp_ss, hp_rs, g_ss, g_rs, e_ss, e_rs, y_ss, y_rs, z_ss, z_rs,
):
    R = len(offsets)
    ROWS = S * R
    HP = conv_ref.shape[1] // 512
    HV = 2 * HP
    L = gu.shape[0]
    D = x_ref.shape[1]
    F = dn.shape[1]
    share = D // E
    g = lax.axis_index("group")
    e = lax.axis_index("ep")

    loads = [
        pltpu.make_async_copy(src, dst, load_sem.at[n])
        for n, (src, dst) in enumerate(
            [(st_hbm, st), (wq_hbm, wq), (wo_hbm, wo), (gu_hbm, gu), (dn_hbm, dn)]
        )
    ]
    for copy in loads:
        copy.start()

    asked = [sgroup_ref[0, j] for j in range(R)]
    request_at = []
    for offset in offsets:
        found = jnp.int32(0)
        for j in range(R):
            found = jnp.where(asked[j] == offset, j, found)
        request_at.append(found)
    slots = [sslot_ref[lax.rem(g + G - offsets[i], G), request_at[i]] for i in range(R)]
    quarter = 16 // S
    width = D // quarter
    own = own_ref[...].astype(f32)
    for j in range(R):
        own32[j, :S, :] = own[j * S : (j + 1) * S]
    for i in range(R):
        four = own32[request_at[i], :S, :]
        tok_ref[16 * i : 16 * (i + 1), :] = jnp.concatenate(
            [four[:, q * width : (q + 1) * width] for q in range(quarter)], axis=0
        ).astype(bf16)
        tail = tail_ref[slots[i]].astype(f32)
        for n in range(3):
            tails_ref[n, i : i + 1, :] = tail[n : n + 1]
    diagonal = lax.broadcasted_iota(jnp.int32, (ROWS, 128), 0) == lax.broadcasted_iota(
        jnp.int32, (ROWS, 128), 1
    )
    wts_ref[...] = jnp.zeros_like(wts_ref)
    for to in range(G):
        for l in range(L):
            named = ids_ref[...] == (to * E + e) * L + l
            weight = jnp.sum(jnp.where(named, probs_ref[...], 0.0), axis=-1, keepdims=True)
            wts_ref[to, l : l + 1, :] = jnp.sum(
                jnp.where(diagonal, weight, 0.0), axis=0, keepdims=True
            )

    barrier = pltpu.get_barrier_semaphore()

    def greet_group(k, carry):
        pl.semaphore_signal(barrier, inc=1, device_id=(lax.rem(g + k, G), e), device_id_type=MESH)
        return carry

    def greet_ep(m, carry):
        pl.semaphore_signal(barrier, inc=1, device_id=(g, lax.rem(e + m, E)), device_id_type=MESH)
        return carry

    lax.fori_loop(1, G, greet_group, 0)
    lax.fori_loop(1, E, greet_ep, 0)
    pl.semaphore_wait(barrier, G - 1 + E - 1)

    def move(src, dst, ss, rs, i, group):
        if offsets[i] % G == 0:
            return pltpu.make_async_copy(src, dst, rs.at[i]), False
        return (
            pltpu.make_async_remote_copy(
                src_ref=src, dst_ref=dst, send_sem=ss.at[i], recv_sem=rs.at[i],
                device_id=(group, e), device_id_type=MESH,
            ),
            True,
        )

    def finish(copies):
        for copy, _ in copies:
            copy.wait()

    tok_copies = []
    for i in range(R):
        rows = pl.ds(16 * i, 16)
        pair = move(tok_ref.at[rows], tok_recv.at[rows], tok_ss, tok_rs, i, lax.rem(g + offsets[i], G))
        pair[0].start()
        tok_copies.append(pair)

    def wts_copy(k):
        to = lax.rem(g + k, G)
        return pltpu.make_async_remote_copy(
            src_ref=wts_ref.at[to], dst_ref=wts_all.at[k], send_sem=w_ss.at[k], recv_sem=w_rs.at[k],
            device_id=(to, e), device_id_type=MESH,
        )

    lax.fori_loop(1, G, lambda k, c: (wts_copy(k).start(), c)[1], 0)
    wts_all[0] = wts_ref[g]

    loads[0].wait()
    st_copies = []
    for i in range(R):
        st_send[i] = st[slots[i]].astype(bf16)
        pair = move(st_send.at[i], st_recv.at[i], st_ss, st_rs, i, lax.rem(g + G - offsets[i], G))
        pair[0].start()
        st_copies.append(pair)

    finish(tok_copies)
    to_row = lax.broadcasted_iota(jnp.int32, (ROWS, 16 * R), 0)
    from_row = lax.broadcasted_iota(jnp.int32, (ROWS, 16 * R), 1)
    for q in range(quarter):
        select = from_row == (to_row % R) * 16 + q * S + to_row // R
        x_ref[:, q * width : (q + 1) * width] = jnp.dot(
            jnp.where(select, 1.0, 0.0).astype(bf16), tok_recv[...], preferred_element_type=f32
        )

    def normalize(x, gain):
        return x * lax.rsqrt(jnp.mean(x * x, axis=-1, keepdims=True) + epsilon) * gain

    nrm[:ROWS] = normalize(x_ref[...], gain_ref[...]).astype(bf16)
    nrm[ROWS:] = normalize(own_ref[...].astype(f32), gain_ref[...]).astype(bf16)

    rates = lax.dot_general(
        nrm[:ROWS], wba_ref[...], (((1,), (1,)), ((), ())), preferred_element_type=f32
    )
    lane = lax.broadcasted_iota(jnp.int32, (1, 4 * HP), 1)
    alog = jnp.zeros((1, 4 * HP), f32)
    dtb = jnp.zeros((1, 4 * HP), f32)
    for head in range(HV):
        here = lane == 4 * (head // 2) + 2 + head % 2
        alog = jnp.where(here, alog_ref[head], alog)
        dtb = jnp.where(here, dtb_ref[head], dtb)
    write_rate = 1.0 / (1.0 + jnp.exp(-rates))
    shifted = rates + dtb
    softplus = jnp.maximum(shifted, 0.0) + jnp.log1p(jnp.exp(-jnp.abs(shifted)))
    decays = jnp.exp(-jnp.exp(alog) * softplus)
    request_of = lax.broadcasted_iota(jnp.int32, (2 * ROWS, 128), 0) % R

    loads[1].wait()
    for h in range(HP):
        projected = jnp.dot(nrm[...], wq[:, h * 768 : (h + 1) * 768], preferred_element_type=f32)
        rounded = projected[:, :512].astype(bf16)
        ct_ref[:, h * 512 : (h + 1) * 512] = rounded[ROWS:].astype(f32)
        entered = rounded[:ROWS].astype(f32)
        window = [tails_ref[n][:, h * 512 : (h + 1) * 512] for n in range(3)]
        window += [entered[s * R : (s + 1) * R] for s in range(S)]
        taps = [conv_ref[n : n + 1, h * 512 : (h + 1) * 512] for n in range(4)]
        ks, qs, vs = [], [], []
        for s in range(S):
            mixed = taps[0] * window[s]
            for n in range(1, 4):
                mixed = mixed + taps[n] * window[s + n]
            out = silu(mixed)
            q_, k_ = out[:, :128], out[:, 128:256]
            qs.append(q_ * lax.rsqrt(jnp.sum(q_ * q_, axis=-1, keepdims=True) + epsilon) * 128 ** (-0.5))
            ks.append(k_ * lax.rsqrt(jnp.sum(k_ * k_, axis=-1, keepdims=True) + epsilon))
            vs.append(out[:, 256:])
        both = jnp.concatenate(ks + qs, axis=0).astype(bf16)
        kk = {(t, s): jnp.sum(ks[t] * ks[s], axis=-1, keepdims=True) for s in range(S) for t in range(s)}
        kq = {(t, s): jnp.sum(ks[t] * qs[s], axis=-1, keepdims=True) for s in range(S) for t in range(s + 1)}
        for s in range(S):
            for i in range(R):
                row = S * HV + h * S + s
                ck_send[i, row : row + 1, :] = ks[s][i : i + 1]
        for p in range(2):
            hv = 2 * h + p

            def apply(i, acc):
                product = jnp.dot(both, st_send[i, hv], preferred_element_type=f32)
                return jnp.where(request_of == i, product, acc)

            start = lax.fori_loop(0, R, apply, jnp.zeros((2 * ROWS, 128), f32))
            dec = [decays[s * R : (s + 1) * R, 4 * h + 2 + p : 4 * h + 3 + p] for s in range(S)]
            beta = [write_rate[s * R : (s + 1) * R, 4 * h + p : 4 * h + p + 1] for s in range(S)]
            kept = []
            total = None
            for s in range(S):
                total = dec[s] if total is None else total * dec[s]
                kept = [c * dec[s] for c in kept]
                guess = total * start[s * R : (s + 1) * R]
                for t in range(s):
                    guess = guess + kk[t, s] * kept[t]
                kept.append(beta[s] * (vs[s][:, p * 128 : (p + 1) * 128] - guess))
                read = total * start[ROWS + s * R : ROWS + (s + 1) * R]
                for t in range(s + 1):
                    read = read + kq[t, s] * kept[t]
                z = projected[s * R : (s + 1) * R, 512 + p * 128 : 640 + p * 128]
                gated[s * R : (s + 1) * R, hv * 128 : (hv + 1) * 128] = (
                    normalize(read, ngain_ref[...]) * silu(z)
                )
            spread = jnp.broadcast_to(total, (R, 128))
            for i in range(R):
                for s in range(S):
                    ck_send[i, hv * S + s : hv * S + s + 1, :] = kept[s][i : i + 1]
                row = S * HV + S * HP + hv
                ck_send[i, row : row + 1, :] = spread[i : i + 1]
    used = S * HV + S * HP + HV
    if used < ck_send.shape[1]:
        for i in range(R):
            ck_send[i, used:, :] = jnp.zeros((ck_send.shape[1] - used, 128), f32)

    loads[2].wait()
    gated16 = gated[...].astype(bf16)
    for q in range(E):
        out = jnp.dot(gated16, wo[:, q * share : (q + 1) * share], preferred_element_type=f32)
        res[q] = x_ref[:, q * share : (q + 1) * share] + out
        hp_send[q] = out.astype(bf16)

    def hp_copy(m):
        return pltpu.make_async_remote_copy(
            src_ref=hp_send, dst_ref=hp_recv.at[m - 1], send_sem=hp_ss.at[m - 1],
            recv_sem=hp_rs.at[m - 1], device_id=(g, lax.rem(e + m, E)), device_id_type=MESH,
        )

    for m in range(1, E):
        hp_copy(m).start()
    ck_copies = []
    for i in range(R):
        pair = move(ck_send.at[i], ck_recv.at[i], ck_ss, ck_rs, i, lax.rem(g + G - offsets[i], G))
        pair[0].start()
        ck_copies.append(pair)
    for m in range(1, E):
        hp_copy(m).wait()
    square = jnp.zeros((ROWS, 1), f32)
    for q in range(E):
        value = res[q]
        for m in range(1, E):
            value = value + hp_recv[m - 1, q].astype(f32)
        res[q] = value
        pgain[q] = pgain_ref[:, q * share : (q + 1) * share]
        square = square + jnp.sum(value * value, axis=-1, keepdims=True)
    scale = lax.rsqrt(square / D + epsilon)

    def rows_of(block):
        return pl.ds(pl.multiple_of(block * ROWS, ROWS), ROWS)

    moe[e, rows_of(g)] = (res[e] * scale * pgain[e]).astype(bf16)

    def group_copy(k):
        place = moe.at[e, rows_of(g)]
        return pltpu.make_async_remote_copy(
            src_ref=place, dst_ref=place, send_sem=g_ss.at[k], recv_sem=g_rs.at[k],
            device_id=(lax.rem(g + k, G), e), device_id_type=MESH,
        )

    def arrived(k):
        place = moe.at[e, rows_of(lax.rem(g + G - k, G))]
        return pltpu.make_async_remote_copy(
            src_ref=place, dst_ref=place, send_sem=g_ss.at[k], recv_sem=g_rs.at[k],
            device_id=(lax.rem(g + k, G), e), device_id_type=MESH,
        )

    def pass_on(k, m):
        place = moe.at[e, rows_of(lax.rem(g + G - k, G))]
        return pltpu.make_async_remote_copy(
            src_ref=place, dst_ref=place, send_sem=e_ss.at[m - 1, k], recv_sem=e_rs.at[m - 1, k],
            device_id=(g, lax.rem(e + m, E)), device_id_type=MESH,
        )

    def taken(k, m):
        place = moe.at[lax.rem(e + E - m, E), rows_of(lax.rem(g + G - k, G))]
        return pltpu.make_async_remote_copy(
            src_ref=place, dst_ref=place, send_sem=e_ss.at[m - 1, k], recv_sem=e_rs.at[m - 1, k],
            device_id=(g, lax.rem(e + m, E)), device_id_type=MESH,
        )

    lax.fori_loop(1, G, lambda k, c: (group_copy(k).start(), c)[1], 0)
    for m in range(1, E):
        pass_on(0, m).start()

    base[...] = jnp.zeros_like(base)
    row_request = lax.broadcasted_iota(jnp.int32, (ROWS, share), 0) % R
    for i in range(R):
        base[lax.rem(g + G - offsets[i], G)] += jnp.where(row_request == i, res[e], 0.0)

    def forward(k, carry):
        arrived(k).wait_recv()
        for m in range(1, E):
            pass_on(k, m).start()
        return carry

    lax.fori_loop(1, G, forward, 0)

    def collect(k, carry):
        for m in range(1, E):
            taken(k, m).wait_recv()
        return carry

    lax.fori_loop(0, G, collect, 0)
    loads[3].wait()
    loads[4].wait()
    for l in range(L):
        halves = jnp.dot(moe[0], gu[l, :share], preferred_element_type=f32)
        for q in range(1, E):
            halves = halves + jnp.dot(
                moe[q], gu[l, q * share : (q + 1) * share], preferred_element_type=f32
            )
        hidden[l] = silu(halves[:, :F]) * halves[:, F:]
    row_hidden = lax.broadcasted_iota(jnp.int32, (ROWS, F), 0) % R

    def regroup(d, carry):
        for l in range(L):
            total = jnp.zeros((ROWS, F), f32)
            for i in range(R):
                total = jnp.where(
                    row_hidden == i, hidden[l, rows_of(lax.rem(d + offsets[i], G))], total
                )
            hid[l, rows_of(d)] = total.astype(bf16)
        return carry

    lax.fori_loop(0, G, regroup, 0)

    lax.fori_loop(1, G, lambda k, c: (wts_copy(k).wait(), c)[1], 0)
    row = lax.broadcasted_iota(jnp.int32, (ROWS, 128), 0)
    wanted = row // R
    for i in range(R):
        wanted = wanted + jnp.where(row % R == i, request_at[i] * S, 0)
    picked = wanted == lax.broadcasted_iota(jnp.int32, (ROWS, 128), 1)
    for q in range(E):
        for l in range(L):
            out = jnp.dot(hid[l], dn[l, :, q * share : (q + 1) * share], preferred_element_type=f32)
            hidden_rows = out.astype(bf16).astype(f32)
            if l == 0:
                sums = [0.0] * G
            for d in range(G):
                tile = wts_all[lax.rem(g + G - d, G)]
                weight = jnp.sum(jnp.where(picked, tile[l : l + 1], 0.0), axis=-1, keepdims=True)
                sums[d] = sums[d] + weight * hidden_rows[d * ROWS : (d + 1) * ROWS]
        for d in range(G):
            y_send[q, d * ROWS : (d + 1) * ROWS] = sums[d].astype(bf16)

    def y_copy(k, m):
        d = lax.rem(g + k, G)
        to = lax.rem(e + m, E)
        return pltpu.make_async_remote_copy(
            src_ref=y_send.at[to, rows_of(d)], dst_ref=y_recv.at[m - 1, rows_of(d)],
            send_sem=y_ss.at[m - 1, k], recv_sem=y_rs.at[m - 1, k],
            device_id=(g, to), device_id_type=MESH,
        )

    def z_copy(k):
        to = lax.rem(g + k, G)
        return pltpu.make_async_remote_copy(
            src_ref=part.at[to], dst_ref=z_recv.at[k], send_sem=z_ss.at[k], recv_sem=z_rs.at[k],
            device_id=(to, e), device_id_type=MESH,
        )

    def y_start(k, carry):
        for m in range(1, E):
            y_copy(lax.rem(k, G), m).start()
        return carry

    lax.fori_loop(1, G + 1, y_start, 0)

    def y_total(k):
        d = lax.rem(g + k, G)
        total = base[d] + y_send[e, rows_of(d)].astype(f32)
        for m in range(1, E):
            y_copy(k, m).wait_recv()
            total = total + y_recv[m - 1, rows_of(d)].astype(f32)
        return total

    def combine(k, carry):
        part[lax.rem(g + k, G)] = y_total(k).astype(bf16)
        z_copy(k).start()
        return carry

    lax.fori_loop(1, G, combine, 0)
    final = y_total(0)

    finish(ck_copies)
    finish(st_copies)

    for k in range(1, G):
        z_copy(k).wait_recv()
        final = final + z_recv[k].astype(f32)
    lay_ref[...] = final

    def drain(k, carry):
        group_copy(k).wait_send()
        z_copy(k).wait_send()
        return carry

    lax.fori_loop(1, G, drain, 0)

    def drain_ep(k, carry):
        for m in range(1, E):
            pass_on(k, m).wait_send()
            y_copy(k, m).wait_send()
        return carry

    lax.fori_loop(0, G, drain_ep, 0)


def body(
    tokens, prefill_states, prefill_tails, src_group, src_slot, in_gain, w_qkvz, w_ba, conv_weight,
    a_log, dt_bias, norm_gain, w_out, post_gain, expert_ids, gate_probs, gate_up_weight, down_weight,
):
    G = lax.axis_size("group")
    E = lax.axis_size("ep")
    g = lax.axis_index("group")
    e = lax.axis_index("ep")
    R, HV = prefill_states.shape[:2]
    ROWS, D = tokens.shape
    S = ROWS // R
    HP = HV // 2
    L = gate_up_weight.shape[0]
    F = down_weight.shape[1]
    C = conv_weight.shape[1]
    share = D // E
    stride = G // R
    offsets = [
        which * stride if stride == 1 or which == R // 2 else (which * stride - 1) % G
        for which in range(R)
    ]
    ck_rows = -(-(S * HV + S * HP + HV) // 8) * 8
    vm = pl.BlockSpec(memory_space=pltpu.VMEM)
    anywhere = pl.BlockSpec(memory_space=pl.ANY)
    dma = pltpu.SemaphoreType.DMA
    V = pltpu.VMEM
    layer, conv_rows, arrived, change = pl.pallas_call(
        functools.partial(kernel, G, E, tuple(offsets), S),
        out_shape=(
            jax.ShapeDtypeStruct((ROWS, share), f32),
            jax.ShapeDtypeStruct((ROWS, C), f32),
            jax.ShapeDtypeStruct(prefill_states.shape, bf16),
            jax.ShapeDtypeStruct((R, ck_rows, 128), f32),
        ),
        in_specs=[pl.BlockSpec(memory_space=pltpu.SMEM)] * 4 + [vm] * 9 + [anywhere] * 5,
        out_specs=(vm, vm, anywhere, anywhere),
        scratch_shapes=[
            V(w_qkvz.shape, bf16), V(w_out.shape, bf16), V(gate_up_weight.shape, bf16),
            V(down_weight.shape, bf16), V(prefill_states.shape, f32),
            V(prefill_states.shape, bf16), V((R, 8, D), f32), V((16 * R, S * D // 16), bf16),
            V((3, R, C), f32), V((G, 8, 128), f32), V((16 * R, S * D // 16), bf16), V((G, 8, 128), f32), V((ROWS, D), f32), V((2 * ROWS, D), bf16),
            V((ROWS, HV * 128), f32), V((R, ck_rows, 128), f32),
            V((E, ROWS, share), bf16), V((E - 1, E, ROWS, share), bf16), V((E, ROWS, share), f32),
            V((E, 1, share), f32),
            V((E, G * ROWS, share), bf16), V((L, G * ROWS, F), f32), V((L, G * ROWS, F), bf16),
            V((E, G * ROWS, share), bf16), V((E - 1, G * ROWS, share), bf16),
            V((G, ROWS, share), f32), V((G, ROWS, share), bf16), V((G, ROWS, share), bf16),
            dma((5,)), dma((R,)), dma((R,)), dma((R,)), dma((R,)), dma((R,)), dma((R,)),
            dma((G,)), dma((G,)), dma((E - 1,)), dma((E - 1,)), dma((G,)), dma((G,)),
            dma((E - 1, G)), dma((E - 1, G)), dma((E - 1, G)), dma((E - 1, G)), dma((G,)), dma((G,)),
        ],
        compiler_params=pltpu.CompilerParams(
            collective_id=0, has_side_effects=True, vmem_limit_bytes=58 * 2**20
        ),
    )(
        src_group, src_slot, a_log, dt_bias, tokens, expert_ids, gate_probs, prefill_tails,
        in_gain.reshape(1, D), w_ba.T, conv_weight, norm_gain.reshape(1, 128),
        post_gain.reshape(1, D), w_qkvz, w_out, gate_up_weight, down_weight, prefill_states,
    )

    def place(j, table):
        found = jnp.int32(0)
        for i, offset in enumerate(offsets):
            found = jnp.where(table[0, j] == offset, i, found)
        return found

    whole = lambda shape: pl.BlockSpec(shape, lambda j, table: (0,) * len(shape))
    layer_out, new_states, new_tails = pl.pallas_call(
        functools.partial(renew, place, S),
        out_shape=(
            jax.ShapeDtypeStruct((ROWS, share), bf16),
            jax.ShapeDtypeStruct(prefill_states.shape, f32),
            jax.ShapeDtypeStruct((R, 3, C), bf16),
        ),
        grid_spec=pltpu.PrefetchScalarGridSpec(
            num_scalar_prefetch=1,
            grid=(R,),
            in_specs=[
                whole((ROWS, share)),
                whole((ROWS, C)),
                pl.BlockSpec((1, HV, 128, 128), lambda j, table: (place(j, table), 0, 0, 0)),
                pl.BlockSpec((1, ck_rows, 128), lambda j, table: (place(j, table), 0, 0)),
            ],
            out_specs=(
                whole((ROWS, share)),
                pl.BlockSpec((1, HV, 128, 128), lambda j, table: (j, 0, 0, 0)),
                whole((R, 3, C)),
            ),
            scratch_shapes=[V((ROWS, share), f32)],
        ),
        compiler_params=pltpu.CompilerParams(vmem_limit_bytes=56 * 2**20),
    )(src_group, layer, conv_rows, arrived, change)
    return (layer_out, new_states, new_tails)


def renew(place, S, table, lay_ref, ct_ref, st_ref, ck_ref, lay_out, st_out, tail_out, ordered):
    R = tail_out.shape[0]
    HV = st_ref.shape[1]
    HP = HV // 2

    @pl.when(pl.program_id(0) == 0)
    def rows():
        for j in range(R):
            i = place(j, table)
            for s in range(S):
                ordered[j * S + s : j * S + s + 1, :] = lay_ref[pl.ds(s * R + i, 1), :]
            tail_out[j] = ct_ref[(j + 1) * S - 3 : (j + 1) * S, :].astype(bf16)
        lay_out[...] = ordered[...].astype(bf16)

    for hv in range(HV):
        h = hv // 2
        k4 = ck_ref[0, S * HV + h * S : S * HV + (h + 1) * S]
        c4 = ck_ref[0, hv * S : (hv + 1) * S]
        row = S * HV + S * HP + hv
        change = lax.dot_general(k4, c4, (((0,), (0,)), ((), ())), preferred_element_type=f32)
        st_out[0, hv] = ck_ref[0, row : row + 1] * st_ref[0, hv].astype(f32) + change


def solution(mesh):
    in_specs = (
        P("group", None), P("group", "ep", None, None), P("group", None, "ep"), P(), P(), P(),
        P(None, "ep"), P(None, "ep"), P(None, "ep"), P("ep"), P("ep"), P(), P("ep", None), P(),
        P("group", None), P("group", None), P(("group", "ep"), None, None),
        P(("group", "ep"), None, None),
    )
    out_specs = (P("group", "ep"), P("group", "ep", None, None), P("group", None, "ep"))
    return jax.shard_map(body, mesh=mesh, in_specs=in_specs, out_specs=out_specs, check_vma=False)
```

```python
import functools
import jax
import jax.numpy as jnp
from jax import lax
from jax.experimental import pallas as pl
from jax.experimental.pallas import tpu as pltpu
from jax.sharding import PartitionSpec as P

epsilon = 1e-06
MESH = pl.DeviceIdType.MESH
bf16, f32 = jnp.bfloat16, jnp.float32


def silu(x):
    return x * (1.0 / (1.0 + jnp.exp(-x)))


def kernel(
    G, E, offsets, S,
    sgroup_ref, sslot_ref, alog_ref, dtb_ref, own_ref, ids_ref, probs_ref, tail_ref, gain_ref, wba_ref,
    conv_ref, ngain_ref, pgain_ref, wq_hbm, wo_hbm, gu_hbm, dn_hbm, st_hbm,
    lay_ref, ct_ref, st_recv, ck_recv,
    wq, wo, gu, dn, st, st_send, own32, tok_ref, tails32, tails_ref, wts_ref, tok_recv, wts_all, x_ref, nrm,
    gated, ck_send, hp_send, hp_recv, res, pgain, moe, hidden, hid, y_send, y_recv, base, part, z_recv,
    load_sem, tok_ss, tok_rs, st_ss, st_rs, ck_ss, ck_rs, w_ss, w_rs,
    hp_ss, hp_rs, g_ss, g_rs, e_ss, e_rs, y_ss, y_rs, z_ss, z_rs,
):
    R = len(offsets)
    ROWS = S * R
    HP = conv_ref.shape[1] // 512
    HV = 2 * HP
    L = gu.shape[0]
    D = x_ref.shape[1]
    F = dn.shape[1]
    share = D // E
    g = lax.axis_index("group")
    e = lax.axis_index("ep")

    loads = [
        pltpu.make_async_copy(src, dst, load_sem.at[n])
        for n, (src, dst) in enumerate(
            [(st_hbm, st), (wq_hbm, wq), (wo_hbm, wo), (gu_hbm, gu), (dn_hbm, dn)]
        )
    ]
    for copy in loads:
        copy.start()

    barrier = pltpu.get_barrier_semaphore()

    def greet_group(k, carry):
        pl.semaphore_signal(barrier, inc=1, device_id=(lax.rem(g + k, G), e), device_id_type=MESH)
        return carry

    def greet_ep(m, carry):
        pl.semaphore_signal(barrier, inc=1, device_id=(g, lax.rem(e + m, E)), device_id_type=MESH)
        return carry

    lax.fori_loop(1, G, greet_group, 0)
    lax.fori_loop(1, E, greet_ep, 0)
    asked = [sgroup_ref[0, j] for j in range(R)]
    request_at = []
    for offset in offsets:
        found = jnp.int32(0)
        for j in range(R):
            found = jnp.where(asked[j] == offset, j, found)
        request_at.append(found)
    slots = [sslot_ref[lax.rem(g + G - offsets[i], G), request_at[i]] for i in range(R)]
    quarter = 16 // S
    width = D // quarter
    tails32[...] = tail_ref[...].astype(f32)
    own = own_ref[...].astype(f32)
    for j in range(R):
        own32[j, :S, :] = own[j * S : (j + 1) * S]
    for i in range(R):
        four = own32[request_at[i], :S, :]
        tok_ref[16 * i : 16 * (i + 1), :] = jnp.concatenate(
            [four[:, q * width : (q + 1) * width] for q in range(quarter)], axis=0
        ).astype(bf16)
        for n in range(3):
            tails_ref[n, i : i + 1, :] = tails32[n, pl.ds(slots[i], 1), :]
    wts_ref[...] = jnp.zeros_like(wts_ref)
    for to in range(G):
        for l in range(L):
            named = ids_ref[...] == (to * E + e) * L + l
            wts_ref[to, l : l + 1, :ROWS] = jnp.sum(
                jnp.where(named, probs_ref[...], 0.0), axis=0, keepdims=True
            )

    pl.semaphore_wait(barrier, G - 1 + E - 1)

    def move(src, dst, ss, rs, i, group):
        if offsets[i] % G == 0:
            return pltpu.make_async_copy(src, dst, rs.at[i]), False
        return (
            pltpu.make_async_remote_copy(
                src_ref=src, dst_ref=dst, send_sem=ss.at[i], recv_sem=rs.at[i],
                device_id=(group, e), device_id_type=MESH,
            ),
            True,
        )

    def finish(copies):
        for copy, _ in copies:
            copy.wait()

    tok_copies = []
    for i in range(R):
        rows = pl.ds(16 * i, 16)
        pair = move(tok_ref.at[rows], tok_recv.at[rows], tok_ss, tok_rs, i, lax.rem(g + offsets[i], G))
        pair[0].start()
        tok_copies.append(pair)

    def wts_copy(k):
        to = lax.rem(g + k, G)
        return pltpu.make_async_remote_copy(
            src_ref=wts_ref.at[to], dst_ref=wts_all.at[k], send_sem=w_ss.at[k], recv_sem=w_rs.at[k],
            device_id=(to, e), device_id_type=MESH,
        )

    lax.fori_loop(1, G, lambda k, c: (wts_copy(k).start(), c)[1], 0)
    wts_all[0] = wts_ref[g]

    loads[0].wait()
    st_copies = []
    for i in range(R):
        st_send[i] = st[slots[i]].astype(bf16)
        pair = move(st_send.at[i], st_recv.at[i], st_ss, st_rs, i, lax.rem(g + G - offsets[i], G))
        pair[0].start()
        st_copies.append(pair)

    finish(tok_copies)
    to_row = lax.broadcasted_iota(jnp.int32, (ROWS, 16 * R), 0)
    from_row = lax.broadcasted_iota(jnp.int32, (ROWS, 16 * R), 1)
    for q in range(quarter):
        select = from_row == (to_row % R) * 16 + q * S + to_row // R
        x_ref[:, q * width : (q + 1) * width] = jnp.dot(
            jnp.where(select, 1.0, 0.0).astype(bf16), tok_recv[...], preferred_element_type=f32
        )

    def normalize(x, gain):
        return x * lax.rsqrt(jnp.mean(x * x, axis=-1, keepdims=True) + epsilon) * gain

    nrm[:ROWS] = normalize(x_ref[...], gain_ref[...]).astype(bf16)
    nrm[ROWS:] = normalize(own_ref[...].astype(f32), gain_ref[...]).astype(bf16)

    rates = lax.dot_general(
        nrm[:ROWS], wba_ref[...], (((1,), (1,)), ((), ())), preferred_element_type=f32
    )
    lane = lax.broadcasted_iota(jnp.int32, (1, 4 * HP), 1)
    alog = jnp.zeros((1, 4 * HP), f32)
    dtb = jnp.zeros((1, 4 * HP), f32)
    for head in range(HV):
        here = lane == 4 * (head // 2) + 2 + head % 2
        alog = jnp.where(here, alog_ref[head], alog)
        dtb = jnp.where(here, dtb_ref[head], dtb)
    write_rate = 1.0 / (1.0 + jnp.exp(-rates))
    shifted = rates + dtb
    softplus = jnp.maximum(shifted, 0.0) + jnp.log1p(jnp.exp(-jnp.abs(shifted)))
    decays = jnp.exp(-jnp.exp(alog) * softplus)
    request_of = lax.broadcasted_iota(jnp.int32, (2 * ROWS, 128), 0) % R

    loads[1].wait()
    for h in range(HP):
        projected = jnp.dot(nrm[...], wq[:, h * 768 : (h + 1) * 768], preferred_element_type=f32)
        rounded = projected[:, :512].astype(bf16)
        ct_ref[:, h * 512 : (h + 1) * 512] = rounded[ROWS:].astype(f32)
        entered = rounded[:ROWS].astype(f32)
        window = [tails_ref[n][:, h * 512 : (h + 1) * 512] for n in range(3)]
        window += [entered[s * R : (s + 1) * R] for s in range(S)]
        taps = [conv_ref[n : n + 1, h * 512 : (h + 1) * 512] for n in range(4)]
        ks, qs, vs = [], [], []
        for s in range(S):
            mixed = taps[0] * window[s]
            for n in range(1, 4):
                mixed = mixed + taps[n] * window[s + n]
            out = silu(mixed)
            q_, k_ = out[:, :128], out[:, 128:256]
            qs.append(q_ * lax.rsqrt(jnp.sum(q_ * q_, axis=-1, keepdims=True) + epsilon) * 128 ** (-0.5))
            ks.append(k_ * lax.rsqrt(jnp.sum(k_ * k_, axis=-1, keepdims=True) + epsilon))
            vs.append(out[:, 256:])
        both = jnp.concatenate(ks + qs, axis=0).astype(bf16)
        kk = {(t, s): jnp.sum(ks[t] * ks[s], axis=-1, keepdims=True) for s in range(S) for t in range(s)}
        kq = {(t, s): jnp.sum(ks[t] * qs[s], axis=-1, keepdims=True) for s in range(S) for t in range(s + 1)}
        for s in range(S):
            for i in range(R):
                row = S * HV + h * S + s
                ck_send[i, row : row + 1, :] = ks[s][i : i + 1]
        for p in range(2):
            hv = 2 * h + p

            def apply(i, acc):
                product = jnp.dot(both, st_send[i, hv], preferred_element_type=f32)
                return jnp.where(request_of == i, product, acc)

            start = lax.fori_loop(0, R, apply, jnp.zeros((2 * ROWS, 128), f32))
            dec = [decays[s * R : (s + 1) * R, 4 * h + 2 + p : 4 * h + 3 + p] for s in range(S)]
            beta = [write_rate[s * R : (s + 1) * R, 4 * h + p : 4 * h + p + 1] for s in range(S)]
            kept = []
            total = None
            for s in range(S):
                total = dec[s] if total is None else total * dec[s]
                kept = [c * dec[s] for c in kept]
                guess = total * start[s * R : (s + 1) * R]
                for t in range(s):
                    guess = guess + kk[t, s] * kept[t]
                kept.append(beta[s] * (vs[s][:, p * 128 : (p + 1) * 128] - guess))
                read = total * start[ROWS + s * R : ROWS + (s + 1) * R]
                for t in range(s + 1):
                    read = read + kq[t, s] * kept[t]
                z = projected[s * R : (s + 1) * R, 512 + p * 128 : 640 + p * 128]
                gated[s * R : (s + 1) * R, hv * 128 : (hv + 1) * 128] = (
                    normalize(read, ngain_ref[...]) * silu(z)
                )
            spread = jnp.broadcast_to(total, (R, 128))
            for i in range(R):
                for s in range(S):
                    ck_send[i, hv * S + s : hv * S + s + 1, :] = kept[s][i : i + 1]
                row = S * HV + S * HP + hv
                ck_send[i, row : row + 1, :] = spread[i : i + 1]
    used = S * HV + S * HP + HV
    if used < ck_send.shape[1]:
        for i in range(R):
            ck_send[i, used:, :] = jnp.zeros((ck_send.shape[1] - used, 128), f32)

    loads[2].wait()
    gated16 = gated[...].astype(bf16)
    for q in range(E):
        out = jnp.dot(gated16, wo[:, q * share : (q + 1) * share], preferred_element_type=f32)
        res[q] = x_ref[:, q * share : (q + 1) * share] + out
        hp_send[q] = out.astype(bf16)

    def hp_copy(m):
        return pltpu.make_async_remote_copy(
            src_ref=hp_send, dst_ref=hp_recv.at[m - 1], send_sem=hp_ss.at[m - 1],
            recv_sem=hp_rs.at[m - 1], device_id=(g, lax.rem(e + m, E)), device_id_type=MESH,
        )

    for m in range(1, E):
        hp_copy(m).start()
    ck_copies = []
    for i in range(R):
        pair = move(ck_send.at[i], ck_recv.at[i], ck_ss, ck_rs, i, lax.rem(g + G - offsets[i], G))
        pair[0].start()
        ck_copies.append(pair)
    for m in range(1, E):
        hp_copy(m).wait()
    square = jnp.zeros((ROWS, 1), f32)
    for q in range(E):
        value = res[q]
        for m in range(1, E):
            value = value + hp_recv[m - 1, q].astype(f32)
        res[q] = value
        pgain[q] = pgain_ref[:, q * share : (q + 1) * share]
        square = square + jnp.sum(value * value, axis=-1, keepdims=True)
    scale = lax.rsqrt(square / D + epsilon)

    def rows_of(block):
        return pl.ds(pl.multiple_of(block * ROWS, ROWS), ROWS)

    moe[e, rows_of(g)] = (res[e] * scale * pgain[e]).astype(bf16)

    def group_copy(k):
        place = moe.at[e, rows_of(g)]
        return pltpu.make_async_remote_copy(
            src_ref=place, dst_ref=place, send_sem=g_ss.at[k], recv_sem=g_rs.at[k],
            device_id=(lax.rem(g + k, G), e), device_id_type=MESH,
        )

    def arrived(k):
        place = moe.at[e, rows_of(lax.rem(g + G - k, G))]
        return pltpu.make_async_remote_copy(
            src_ref=place, dst_ref=place, send_sem=g_ss.at[k], recv_sem=g_rs.at[k],
            device_id=(lax.rem(g + k, G), e), device_id_type=MESH,
        )

    def pass_on(k, m):
        place = moe.at[e, rows_of(lax.rem(g + G - k, G))]
        return pltpu.make_async_remote_copy(
            src_ref=place, dst_ref=place, send_sem=e_ss.at[m - 1, k], recv_sem=e_rs.at[m - 1, k],
            device_id=(g, lax.rem(e + m, E)), device_id_type=MESH,
        )

    def taken(k, m):
        place = moe.at[lax.rem(e + E - m, E), rows_of(lax.rem(g + G - k, G))]
        return pltpu.make_async_remote_copy(
            src_ref=place, dst_ref=place, send_sem=e_ss.at[m - 1, k], recv_sem=e_rs.at[m - 1, k],
            device_id=(g, lax.rem(e + m, E)), device_id_type=MESH,
        )

    lax.fori_loop(1, G, lambda k, c: (group_copy(k).start(), c)[1], 0)
    for m in range(1, E):
        pass_on(0, m).start()

    base[...] = jnp.zeros_like(base)
    row_request = lax.broadcasted_iota(jnp.int32, (ROWS, share), 0) % R
    for i in range(R):
        base[lax.rem(g + G - offsets[i], G)] += jnp.where(row_request == i, res[e], 0.0)

    def forward(k, carry):
        arrived(k).wait_recv()
        for m in range(1, E):
            pass_on(k, m).start()
        return carry

    lax.fori_loop(1, G, forward, 0)

    def collect(k, carry):
        for m in range(1, E):
            taken(k, m).wait_recv()
        return carry

    lax.fori_loop(0, G, collect, 0)
    loads[3].wait()
    loads[4].wait()
    for l in range(L):
        halves = jnp.dot(moe[0], gu[l, :share], preferred_element_type=f32)
        for q in range(1, E):
            halves = halves + jnp.dot(
                moe[q], gu[l, q * share : (q + 1) * share], preferred_element_type=f32
            )
        hidden[l] = silu(halves[:, :F]) * halves[:, F:]
    row_hidden = lax.broadcasted_iota(jnp.int32, (ROWS, F), 0) % R

    def regroup(d, carry):
        for l in range(L):
            total = jnp.zeros((ROWS, F), f32)
            for i in range(R):
                total = jnp.where(
                    row_hidden == i, hidden[l, rows_of(lax.rem(d + offsets[i], G))], total
                )
            hid[l, rows_of(d)] = total.astype(bf16)
        return carry

    lax.fori_loop(0, G, regroup, 0)

    lax.fori_loop(1, G, lambda k, c: (wts_copy(k).wait(), c)[1], 0)
    row = lax.broadcasted_iota(jnp.int32, (ROWS, 128), 0)
    wanted = row // R
    for i in range(R):
        wanted = wanted + jnp.where(row % R == i, request_at[i] * S, 0)
    picked = wanted == lax.broadcasted_iota(jnp.int32, (ROWS, 128), 1)
    for q in range(E):
        for l in range(L):
            out = jnp.dot(hid[l], dn[l, :, q * share : (q + 1) * share], preferred_element_type=f32)
            hidden_rows = out.astype(bf16).astype(f32)
            if l == 0:
                sums = [0.0] * G
            for d in range(G):
                tile = wts_all[lax.rem(g + G - d, G)]
                weight = jnp.sum(jnp.where(picked, tile[l : l + 1], 0.0), axis=-1, keepdims=True)
                sums[d] = sums[d] + weight * hidden_rows[d * ROWS : (d + 1) * ROWS]
        for d in range(G):
            y_send[q, d * ROWS : (d + 1) * ROWS] = sums[d].astype(bf16)

    def y_copy(k, m):
        d = lax.rem(g + k, G)
        to = lax.rem(e + m, E)
        return pltpu.make_async_remote_copy(
            src_ref=y_send.at[to, rows_of(d)], dst_ref=y_recv.at[m - 1, rows_of(d)],
            send_sem=y_ss.at[m - 1, k], recv_sem=y_rs.at[m - 1, k],
            device_id=(g, to), device_id_type=MESH,
        )

    def z_copy(k):
        to = lax.rem(g + k, G)
        return pltpu.make_async_remote_copy(
            src_ref=part.at[to], dst_ref=z_recv.at[k], send_sem=z_ss.at[k], recv_sem=z_rs.at[k],
            device_id=(to, e), device_id_type=MESH,
        )

    def y_start(k, carry):
        for m in range(1, E):
            y_copy(lax.rem(k, G), m).start()
        return carry

    lax.fori_loop(1, G + 1, y_start, 0)

    def y_total(k):
        d = lax.rem(g + k, G)
        total = base[d] + y_send[e, rows_of(d)].astype(f32)
        for m in range(1, E):
            y_copy(k, m).wait_recv()
            total = total + y_recv[m - 1, rows_of(d)].astype(f32)
        return total

    def combine(k, carry):
        part[lax.rem(g + k, G)] = y_total(k).astype(bf16)
        z_copy(k).start()
        return carry

    lax.fori_loop(1, G, combine, 0)
    final = y_total(0)

    finish(ck_copies)
    finish(st_copies)

    for k in range(1, G):
        z_copy(k).wait_recv()
        final = final + z_recv[k].astype(f32)
    lay_ref[...] = final

    def drain(k, carry):
        group_copy(k).wait_send()
        z_copy(k).wait_send()
        return carry

    lax.fori_loop(1, G, drain, 0)

    def drain_ep(k, carry):
        for m in range(1, E):
            pass_on(k, m).wait_send()
            y_copy(k, m).wait_send()
        return carry

    lax.fori_loop(0, G, drain_ep, 0)


def body(
    tokens, prefill_states, prefill_tails, src_group, src_slot, in_gain, w_qkvz, w_ba, conv_weight,
    a_log, dt_bias, norm_gain, w_out, post_gain, expert_ids, gate_probs, gate_up_weight, down_weight,
):
    G = lax.axis_size("group")
    E = lax.axis_size("ep")
    g = lax.axis_index("group")
    e = lax.axis_index("ep")
    R, HV = prefill_states.shape[:2]
    ROWS, D = tokens.shape
    S = ROWS // R
    HP = HV // 2
    L = gate_up_weight.shape[0]
    F = down_weight.shape[1]
    C = conv_weight.shape[1]
    share = D // E
    stride = G // R
    offsets = [
        which * stride if stride == 1 or which == R // 2 else (which * stride - 1) % G
        for which in range(R)
    ]
    ck_rows = -(-(S * HV + S * HP + HV) // 8) * 8
    vm = pl.BlockSpec(memory_space=pltpu.VMEM)
    anywhere = pl.BlockSpec(memory_space=pl.ANY)
    dma = pltpu.SemaphoreType.DMA
    V = pltpu.VMEM
    layer, conv_rows, arrived, change = pl.pallas_call(
        functools.partial(kernel, G, E, tuple(offsets), S),
        out_shape=(
            jax.ShapeDtypeStruct((ROWS, share), f32),
            jax.ShapeDtypeStruct((ROWS, C), f32),
            jax.ShapeDtypeStruct(prefill_states.shape, bf16),
            jax.ShapeDtypeStruct((R, ck_rows, 128), f32),
        ),
        in_specs=[pl.BlockSpec(memory_space=pltpu.SMEM)] * 4 + [vm] * 9 + [anywhere] * 5,
        out_specs=(vm, vm, anywhere, anywhere),
        scratch_shapes=[
            V(w_qkvz.shape, bf16), V(w_out.shape, bf16), V(gate_up_weight.shape, bf16),
            V(down_weight.shape, bf16), V(prefill_states.shape, f32),
            V(prefill_states.shape, bf16), V((R, 8, D), f32), V((16 * R, S * D // 16), bf16),
            V((3, R, C), f32), V((3, R, C), f32), V((G, 8, 128), f32), V((16 * R, S * D // 16), bf16), V((G, 8, 128), f32), V((ROWS, D), f32), V((2 * ROWS, D), bf16),
            V((ROWS, HV * 128), f32), V((R, ck_rows, 128), f32),
            V((E, ROWS, share), bf16), V((E - 1, E, ROWS, share), bf16), V((E, ROWS, share), f32),
            V((E, 1, share), f32),
            V((E, G * ROWS, share), bf16), V((L, G * ROWS, F), f32), V((L, G * ROWS, F), bf16),
            V((E, G * ROWS, share), bf16), V((E - 1, G * ROWS, share), bf16),
            V((G, ROWS, share), f32), V((G, ROWS, share), bf16), V((G, ROWS, share), bf16),
            dma((5,)), dma((R,)), dma((R,)), dma((R,)), dma((R,)), dma((R,)), dma((R,)),
            dma((G,)), dma((G,)), dma((E - 1,)), dma((E - 1,)), dma((G,)), dma((G,)),
            dma((E - 1, G)), dma((E - 1, G)), dma((E - 1, G)), dma((E - 1, G)), dma((G,)), dma((G,)),
        ],
        compiler_params=pltpu.CompilerParams(
            collective_id=0, has_side_effects=True, vmem_limit_bytes=58 * 2**20
        ),
    )(
        src_group, src_slot, a_log, dt_bias, tokens, expert_ids.T, gate_probs.T,
        prefill_tails.transpose(1, 0, 2),
        in_gain.reshape(1, D), w_ba.T, conv_weight, norm_gain.reshape(1, 128),
        post_gain.reshape(1, D), w_qkvz, w_out, gate_up_weight, down_weight, prefill_states,
    )

    def place(j, table):
        found = jnp.int32(0)
        for i, offset in enumerate(offsets):
            found = jnp.where(table[0, j] == offset, i, found)
        return found

    whole = lambda shape: pl.BlockSpec(shape, lambda j, table: (0,) * len(shape))
    layer_out, new_states, new_tails = pl.pallas_call(
        functools.partial(renew, place, S),
        out_shape=(
            jax.ShapeDtypeStruct((ROWS, share), bf16),
            jax.ShapeDtypeStruct(prefill_states.shape, f32),
            jax.ShapeDtypeStruct((3, R, C), bf16),
        ),
        grid_spec=pltpu.PrefetchScalarGridSpec(
            num_scalar_prefetch=1,
            grid=(R,),
            in_specs=[
                whole((ROWS, share)),
                whole((ROWS, C)),
                pl.BlockSpec((1, HV, 128, 128), lambda j, table: (place(j, table), 0, 0, 0)),
                pl.BlockSpec((1, ck_rows, 128), lambda j, table: (place(j, table), 0, 0)),
            ],
            out_specs=(
                whole((ROWS, share)),
                pl.BlockSpec((1, HV, 128, 128), lambda j, table: (j, 0, 0, 0)),
                whole((3, R, C)),
            ),
            scratch_shapes=[V((ROWS, share), f32), V((3, R, C), f32)],
        ),
        compiler_params=pltpu.CompilerParams(vmem_limit_bytes=56 * 2**20),
    )(src_group, layer, conv_rows, arrived, change)
    return (layer_out, new_states, new_tails.transpose(1, 0, 2))


def renew(place, S, table, lay_ref, ct_ref, st_ref, ck_ref, lay_out, st_out, tail_out, ordered, last):
    R = tail_out.shape[1]
    HV = st_ref.shape[1]
    HP = HV // 2

    @pl.when(pl.program_id(0) == 0)
    def rows():
        for j in range(R):
            i = place(j, table)
            for s in range(S):
                ordered[j * S + s : j * S + s + 1, :] = lay_ref[pl.ds(s * R + i, 1), :]
            for n in range(3):
                row = (j + 1) * S - 3 + n
                last[n, j : j + 1, :] = ct_ref[row : row + 1, :]
        tail_out[...] = last[...].astype(bf16)
        lay_out[...] = ordered[...].astype(bf16)

    for hv in range(HV):
        h = hv // 2
        k4 = ck_ref[0, S * HV + h * S : S * HV + (h + 1) * S]
        c4 = ck_ref[0, hv * S : (hv + 1) * S]
        row = S * HV + S * HP + hv
        change = lax.dot_general(k4, c4, (((0,), (0,)), ((), ())), preferred_element_type=f32)
        st_out[0, hv] = ck_ref[0, row : row + 1] * st_ref[0, hv].astype(f32) + change


def solution(mesh):
    in_specs = (
        P("group", None), P("group", "ep", None, None), P("group", None, "ep"), P(), P(), P(),
        P(None, "ep"), P(None, "ep"), P(None, "ep"), P("ep"), P("ep"), P(), P("ep", None), P(),
        P("group", None), P("group", None), P(("group", "ep"), None, None),
        P(("group", "ep"), None, None),
    )
    out_specs = (P("group", "ep"), P("group", "ep", None, None), P("group", None, "ep"))
    return jax.shard_map(body, mesh=mesh, in_specs=in_specs, out_specs=out_specs, check_vma=False)
```
